256 devices in a mesh: row: 32 (over y_hi, z, core), col: 8 (over x, y_lo).
Axes of the slice: x: 4, y: 4 (y_hi: 2, y_lo: 2; y = y_hi * 2 + y_lo), z: 8, core: 2. Of those that a mesh axis runs over, the one named last changes fastest.
Arguments:
- pair: bfloat16 [512, 512, 128], P('row', 'col'), may hold values from -6 to 6
- in_gain: float32 [2, 128], replicated, may hold values from 0.25 to 1.75
- in_bias: float32 [2, 128], replicated, may hold values from -2 to 2
- projection: bfloat16 [2, 128, 640], replicated, may hold values from -0.5 to 0.5
- out_gain: float32 [2, 128], replicated, may hold values from 0.25 to 1.75
- out_bias: float32 [2, 128], replicated, may hold values from -2 to 2
- out_weight: bfloat16 [2, 128, 128], replicated, may hold values from -0.5 to 0.5
Outputs:
- updated: bfloat16 [512, 512, 128], P('row', 'col')
The draws below stay inside these ranges and needn't reach their ends.
All inputs are finite; a program needn't handle non-finite values.
Results may differ from the reference program's by a relative error of at most 0.014.
Values may be sent and summed in bfloat16 or wider, within the bound.
A program may use at most 64 MiB of HBM per device.

```python
import jax
import jax.numpy as jnp
from jax import lax

C = 128
H = 128
TOKENS = 512


def level_of(stream_key, extent, cuts, low, high):
    def one(position, shards_of):
        steps = jax.random.uniform(jax.random.fold_in(jax.random.fold_in(stream_key, 6), position), (shards_of,), jnp.float32, low / len(cuts), high / len(cuts))
        return jnp.repeat(jnp.exp(steps), extent[position] // shards_of).reshape((-1,) + (1,) * (len(extent) - position - 1))

    factor_of = one(*cuts[0])
    for cut in cuts[1:]:
        factor_of = factor_of * one(*cut)
    return factor_of


def gaussian(rng, shape, spread, limit, pieces=(), kind=jnp.bfloat16):
    values = jax.random.normal(rng, shape, jnp.float32) * spread
    if len(pieces) > 0:
        values = level_of(rng, shape, pieces, -0.22, 0.18) * values
    return jnp.clip(values, min=-limit, max=limit).astype(kind)


def setup_inputs(seed: int = 0) -> dict:
    key_of = jax.random.split(jax.random.key(seed), 8)
    return {
        "pair": gaussian(key_of[0], (TOKENS, TOKENS, C), 1.0, 6.0, ((0, 32), (1, 8))),
        "in_gain": jnp.clip(1.0 + 0.15 * jax.random.normal(key_of[1], (2, C), jnp.float32), 0.25, 1.75),
        "in_bias": gaussian(key_of[2], (2, C), 0.4, 2.0, (), jnp.float32),
        "projection": gaussian(key_of[3], (2, C, 4 * H + C), C ** -0.5, 0.5),
        "out_gain": jnp.clip(1.0 + 0.15 * jax.random.normal(key_of[4], (2, H), jnp.float32), 0.25, 1.75),
        "out_bias": gaussian(key_of[5], (2, H), 0.4, 2.0, (), jnp.float32),
        "out_weight": gaussian(key_of[6], (2, H, C), H ** -0.5, 0.5),
    }


def layer_norm(values, gain, offset):
    mean = lax.optimization_barrier(jnp.mean(values, axis=-1, keepdims=True))
    centred = values - mean
    var = lax.optimization_barrier(jnp.mean(centred * centred, axis=-1, keepdims=True))
    return centred / jnp.sqrt(var + 1e-05) * gain + offset

def one_update(state, which, in_gain, in_bias, projection, out_gain, out_bias, out_weight):
    count = state.shape[0]
    normed = layer_norm(state.astype(jnp.float32), in_gain[which], in_bias[which]).astype(jnp.bfloat16)
    proj = jnp.dot(normed.reshape(count * count, C), projection[which], preferred_element_type=jnp.float32)
    proj = proj.reshape(count, count, 4 * H + C)
    left = (jax.nn.sigmoid(proj[..., H:2 * H]) * proj[..., :H]).astype(jnp.bfloat16)
    right = (jax.nn.sigmoid(proj[..., 3 * H:4 * H]) * proj[..., 2 * H:3 * H]).astype(jnp.bfloat16)
    gate = jax.nn.sigmoid(proj[..., 4 * H:])
    if which == 0:
        tri = jnp.einsum('ikh,jkh->ijh', left.astype(jnp.float32), right.astype(jnp.float32))
    else:
        tri = jnp.einsum('kih,kjh->ijh', left.astype(jnp.float32), right.astype(jnp.float32))
    normtri = layer_norm(tri, out_gain[which], out_bias[which]).astype(jnp.bfloat16)
    delta = jnp.dot(normtri.reshape(count * count, H), out_weight[which], preferred_element_type=jnp.float32)
    delta = delta.reshape(count, count, C)
    return (state.astype(jnp.float32) + gate * delta).astype(jnp.bfloat16)

def reference(pair, in_gain, in_bias, projection, out_gain, out_bias, out_weight):
    state1 = one_update(pair, 0, in_gain, in_bias, projection, out_gain, out_bias, out_weight)
    return one_update(state1, 1, in_gain, in_bias, projection, out_gain, out_bias, out_weight)
```

```python
import jax
import jax.numpy as jnp
from jax import lax
from jax.experimental import pallas as pl
from jax.experimental.pallas import tpu as pltpu
from jax.sharding import PartitionSpec as P

F32 = jnp.float32
BF16 = jnp.bfloat16
C = 128
H = 128
ROWS = 16
COLS = 64
LANES = ROWS * COLS
NZ = 8
NP = 16
GROUP = 2
NG = NZ // GROUP
STEPS = (0, 1, 7, 2, 6, 3, 5, 4)
BACK = (4, 3, 5, 2, 6, 1, 7, 0)
EPS = 1e-05


def column(row):
    eye = lax.broadcasted_iota(jnp.int32, (C, C), 0) == lax.broadcasted_iota(jnp.int32, (C, C), 1)
    return jnp.sum(jnp.where(eye, jnp.broadcast_to(row, (C, C)), 0.0), axis=1, keepdims=True)


def norm0(values, gain, offset):
    mean = jnp.sum(values, axis=0, keepdims=True) * (1.0 / C)
    centred = values - mean
    var = jnp.sum(centred * centred, axis=0, keepdims=True) * (1.0 / C)
    return centred * lax.rsqrt(var + EPS) * gain + offset


def sigmoid(x):
    return 0.5 * jnp.tanh(0.5 * x) + 0.5


def dot(a, b, dims):
    return lax.dot_general(a, b, (dims, ((), ())), preferred_element_type=F32)


def kernel(
    pair, in_gain, in_bias, projection, out_gain, out_bias, out_weight, updated,
    state, normed, gate, cols, wt, wo,
    sa, ra, spread, sx, rx, am, at, bm, tx, ty, tz, tf,
    s1, r1, s2, r2, s3, r3, s4, r4, s5, r5,
):
    row = lax.axis_index("row")
    col = lax.axis_index("col")
    core = row % 2
    z = (row // 2) % NZ
    yh = row // (2 * NZ)
    p = col * 2 + yh

    def zdev(zz):
        return ((yh * NZ + zz) * 2 + core, col)

    def pdev(pp):
        return (((pp % 2) * NZ + z) * 2 + core, pp // 2)

    sibling = (row - core + (1 - core), col)

    barrier = pltpu.get_barrier_semaphore()

    def greet_z(d, _):
        pl.semaphore_signal(barrier, 1, device_id=zdev((z + d) % NZ), device_id_type=pl.DeviceIdType.MESH)
        return 0

    def greet_p(d, _):
        pl.semaphore_signal(barrier, 1, device_id=pdev((p + d) % NP), device_id_type=pl.DeviceIdType.MESH)
        return 0

    lax.fori_loop(1, NZ, greet_z, 0)
    lax.fori_loop(1, NP, greet_p, 0)
    pl.semaphore_signal(barrier, 1, device_id=sibling, device_id_type=pl.DeviceIdType.MESH)

    def remote(src, dst, send, recv, device):
        return pltpu.make_async_remote_copy(
            src_ref=src, dst_ref=dst, send_sem=send, recv_sem=recv,
            device_id=device, device_id_type=pl.DeviceIdType.MESH,
        )

    low = lax.broadcasted_iota(jnp.int32, (1, 128), 1) < COLS

    def swap(x):
        return pltpu.roll(x, COLS, 1)

    for t in range(8):
        tile = jnp.concatenate([pair[t], pair[t + 8]], axis=0).astype(F32)
        state[:, t * 128:(t + 1) * 128] = tile.T
    for u in range(2):
        for n, ref in enumerate((in_gain, in_bias, out_gain, out_bias)):
            cols[u, n] = jnp.broadcast_to(column(ref[u:u + 1, :]), (C, 128))
        for g in range(5):
            wt[u, g * 128:(g + 1) * 128, :] = projection[u, :, g * 128:(g + 1) * 128].astype(F32).T.astype(BF16)
        wo[u] = out_weight[u].astype(F32).T.astype(BF16)

    pl.semaphore_wait(barrier, NZ - 1 + NP - 1 + 1)

    for u in range(2):
        def project(t, _):
            lanes = pl.ds(pl.multiple_of(t * 128, 128), 128)
            nrm = norm0(state[:, lanes], cols[u, 0], cols[u, 1]).astype(BF16)
            normed[:, lanes] = nrm
            proj = dot(wt[u, :512, :], nrm, ((1,), (0,)))
            left = (sigmoid(proj[128:256]) * proj[:128]).astype(BF16)
            right = (sigmoid(proj[384:512]) * proj[256:384]).astype(BF16)
            sa[u, :, 0:16, lanes] = left.reshape(NZ, 16, 128)
            sa[u, :, 16:32, lanes] = right.reshape(NZ, 16, 128)
            return 0

        lax.fori_loop(0, 8, project, 0)

        for d in (4, 3, 5, 2, 6, 1, 7):
            to = (z + d) % NZ
            remote(sa.at[u, to], ra.at[u, z], s1.at[u, d], r1.at[u, z], zdev(to)).start()

        def gates(t, _):
            lanes = pl.ds(pl.multiple_of(t * 128, 128), 128)
            gate[:, lanes] = sigmoid(dot(wt[u, 512:, :], normed[:, lanes], ((1,), (0,))))
            return 0

        lax.fori_loop(0, 8, gates, 0)

        def spread_out(s):
            zs = (z + STEPS[s]) % NZ
            if s > 0:
                remote(sa.at[u, zs], ra.at[u, zs], s1.at[u, 0], r1.at[u, zs], zdev(zs)).wait_recv()
            src = sa.at[u, zs] if s == 0 else ra.at[u, zs]
            for t in range(8):
                vl = src[0:16, t * 128:(t + 1) * 128].astype(F32)
                vr = src[16:32, t * 128:(t + 1) * 128].astype(F32)
                spread[pl.ds(t, 16, stride=16), :] = jnp.where(low, vl, swap(vr))
                spread[pl.ds(8 + t, 16, stride=16), :] = jnp.where(low, swap(vl), vr)
            sx[u, :, s] = spread[...].reshape(NP, 16, 128).astype(BF16)

        def send_plane(g):
            steps = pl.ds(g * GROUP, GROUP)
            pltpu.make_async_copy(sx.at[u, p, steps], rx.at[u, col, yh, core, steps], r2.at[u, g]).start()

            def one(d, _):
                to = (p + d) % NP
                remote(sx.at[u, to, steps], rx.at[u, col, yh, core, steps], s2.at[u, g], r2.at[u, g], pdev(to)).start()
                return 0

            lax.fori_loop(1, NP, one, 0)

        def swap_cores(g):
            steps = pl.ds(g * GROUP, GROUP)
            whole = rx.at[u, :, :, core, steps]
            pltpu.make_async_copy(whole, whole, r2.at[u, g]).wait()
            remote(whole, whole, s3.at[u, g], r3.at[u, g], sibling).start()

        def build(g):
            steps = pl.ds(g * GROUP, GROUP)
            other = rx.at[u, :, :, 1 - core, steps]
            pltpu.make_async_copy(other, other, r3.at[u, g]).wait()
            for s in range(g * GROUP, (g + 1) * GROUP):
                zs = (z + STEPS[s]) % NZ
                for h in range(2):
                    for k in range(2):
                        place = pl.ds(pl.multiple_of(((h * NZ + zs) * 2 + k) * 16, 16), 16)
                        for c in range(4):
                            x0 = rx[u, 2 * c, h, k, s].astype(F32)
                            x1 = rx[u, 2 * c + 1, h, k, s].astype(F32)
                            am[place, c * 128:(c + 1) * 128] = jnp.where(low, x0, swap(x1)).astype(BF16)
                            bm[place, c * 128:(c + 1) * 128] = jnp.where(low, swap(x0), x1).astype(BF16)

        for g in range(NG):
            for s in range(g * GROUP, (g + 1) * GROUP):
                spread_out(s)
            send_plane(g)
            if g > 0:
                swap_cores(g - 1)
            if g > 1:
                build(g - 2)
        swap_cores(NG - 1)
        build(NG - 2)
        build(NG - 1)

        if u == 1:
            def flip(i, _):
                lanes = pl.ds(pl.multiple_of(i * 128, 128), 128)
                for k in range(4):
                    at[lanes, k * 128:(k + 1) * 128] = am[k * 128:(k + 1) * 128, lanes].astype(F32).T.astype(BF16)
                return 0

            lax.fori_loop(0, 4, flip, 0)
        a_ref = am if u == 0 else at

        def triangle(g):
            rows = []
            for s in BACK[g * GROUP:(g + 1) * GROUP]:
                for h in range(2):
                    r = ((h * NZ + (z + s) % NZ) * 2 + core) * 16
                    rows.append(a_ref[pl.ds(pl.multiple_of(r, 16), 16), :])
            tri = dot(jnp.concatenate(rows, axis=0), bm[...], ((1,), (1 - u,)))
            for h in range(2):
                for c in range(4):
                    first, second = [], []
                    for s in range(GROUP):
                        block = tri[(s * 2 + h) * 16:(s * 2 + h + 1) * 16, c * 128:(c + 1) * 128]
                        first.append(jnp.where(low, block[0:8], swap(block[8:16])))
                        second.append(jnp.where(low, swap(block[0:8]), block[8:16]))
                    tx[u, g, 4 * c + h] = jnp.concatenate(first, axis=0).astype(BF16)
                    tx[u, g, 4 * c + 2 + h] = jnp.concatenate(second, axis=0).astype(BF16)

        def send_back(g):
            pltpu.make_async_copy(tx.at[u, g, p], ty.at[u, g, p], r4.at[u, g]).start()

            def one(d, _):
                to = (p + d) % NP
                remote(tx.at[u, g, to], ty.at[u, g, p], s4.at[u, g], r4.at[u, g], pdev(to)).start()
                return 0

            lax.fori_loop(1, NP, one, 0)

        def gather_back(g):
            whole = ty.at[u, g]
            pltpu.make_async_copy(whole, whole, r4.at[u, g]).wait()
            for h in range(NP):
                spread[pl.ds(h, 16, stride=16), :] = ty[u, g, h].astype(F32)
            for n in range(GROUP):
                d = BACK[g * GROUP + n]
                for t in range(8):
                    at_row = (n * 8 + t) * 16
                    tile = spread[at_row:at_row + 16, :].astype(BF16)
                    if d == 0:
                        tf[u, z, :, t * 128:(t + 1) * 128] = tile
                    else:
                        tz[u, d, :, t * 128:(t + 1) * 128] = tile
                if d:
                    remote(tz.at[u, d], tf.at[u, z], s5.at[u, d], r5.at[u, z], zdev((z + d) % NZ)).start()

        for g in range(NG):
            triangle(g)
            send_back(g)
            if g > 0:
                gather_back(g - 1)
        gather_back(NG - 1)

        for d in range(1, NZ):
            zs = (z + d) % NZ
            remote(tz.at[u, d], tf.at[u, zs], s5.at[u, d], r5.at[u, zs], zdev(zs)).wait_recv()

        def finish(t, _):
            lanes = pl.ds(pl.multiple_of(t * 128, 128), 128)
            tri = tf[u, :, :, lanes].reshape(H, 128).astype(F32)
            nrm = norm0(tri, cols[u, 2], cols[u, 3]).astype(BF16)
            delta = dot(wo[u], nrm, ((1,), (0,)))
            new = state[:, lanes] + gate[:, lanes] * delta
            if u == 0:
                state[:, lanes] = new.astype(BF16).astype(F32)
            else:
                tile = new.T.astype(BF16)
                updated[t] = tile[0:COLS]
                updated[t + 8] = tile[COLS:]
            return 0

        lax.fori_loop(0, 8, finish, 0)

    for u in range(2):
        for d in range(1, NZ):
            zs = (z + d) % NZ
            remote(sa.at[u, zs], ra.at[u, z], s1.at[u, d], r1.at[u, z], zdev(zs)).wait_send()
            remote(tz.at[u, d], tf.at[u, z], s5.at[u, d], r5.at[u, z], zdev(zs)).wait_send()
        for g in range(NG):
            sent = sx.at[u, pl.ds(0, NP - 1), pl.ds(g * GROUP, GROUP)]
            pltpu.make_async_copy(sent, sent, s2.at[u, g]).wait()
            sent = tx.at[u, g, pl.ds(0, NP - 1)]
            pltpu.make_async_copy(sent, sent, s4.at[u, g]).wait()
            sent = rx.at[u, :, :, core, pl.ds(g * GROUP, GROUP)]
            pltpu.make_async_copy(sent, sent, s3.at[u, g]).wait()


def local(pair, in_gain, in_bias, projection, out_gain, out_bias, out_weight):
    vm = pltpu.VMEM
    dma = pltpu.SemaphoreType.DMA
    return pl.pallas_call(
        kernel,
        out_shape=jax.ShapeDtypeStruct((ROWS, COLS, C), BF16),
        in_specs=[pl.BlockSpec(memory_space=vm)] * 7,
        out_specs=pl.BlockSpec(memory_space=vm),
        scratch_shapes=[
            vm((C, LANES), F32),
            vm((C, LANES), BF16),
            vm((C, LANES), F32),
            vm((2, 4, C, 128), F32),
            vm((2, 640, C), BF16),
            vm((2, C, H), BF16),
            vm((2, NZ, 32, LANES), BF16),
            vm((2, NZ, 32, LANES), BF16),
            vm((256, 128), F32),
            vm((2, NP, NZ, 16, 128), BF16),
            vm((2, 8, 2, 2, NZ, 16, 128), BF16),
            vm((512, 512), BF16),
            vm((512, 512), BF16),
            vm((512, 512), BF16),
            vm((2, NG, NP, 16, 128), BF16),
            vm((2, NG, NP, 16, 128), BF16),
            vm((2, NZ, 16, LANES), BF16),
            vm((2, NZ, 16, LANES), BF16),
            dma((2, NZ)), dma((2, NZ)),
            dma((2, NG)), dma((2, NG)),
            dma((2, NG)), dma((2, NG)),
            dma((2, NG)), dma((2, NG)),
            dma((2, NZ)), dma((2, NZ)),
        ],
        compiler_params=pltpu.CompilerParams(
            collective_id=0, has_side_effects=True, vmem_limit_bytes=40 * 1024 * 1024
        ),
    )(pair, in_gain, in_bias, projection, out_gain, out_bias, out_weight)


def solution(mesh):
    return jax.shard_map(
        local,
        mesh=mesh,
        in_specs=(P("row", "col", None), P(), P(), P(), P(), P(), P()),
        out_specs=P("row", "col", None),
        check_vma=False,
    )
```

```python
import jax
import jax.numpy as jnp
from jax import lax
from jax.experimental import pallas as pl
from jax.experimental.pallas import tpu as pltpu
from jax.sharding import PartitionSpec as P

F32 = jnp.float32
BF16 = jnp.bfloat16
C = 128
H = 128
ROWS = 16
COLS = 64
LANES = ROWS * COLS
NZ = 8
NP = 16
GROUP = 2
NG = NZ // GROUP
STEPS = (0, 1, 7, 2, 6, 3, 5, 4)
PLANE = (10, 6, 9, 11, 14, 2, 8, 5, 7, 13, 15, 1, 3, 4, 12)
BACK = (4, 3, 5, 2, 6, 1, 7, 0)
EPS = 1e-05


def column(row):
    eye = lax.broadcasted_iota(jnp.int32, (C, C), 0) == lax.broadcasted_iota(jnp.int32, (C, C), 1)
    return jnp.sum(jnp.where(eye, jnp.broadcast_to(row, (C, C)), 0.0), axis=1, keepdims=True)


def norm0(values, gain, offset):
    mean = jnp.sum(values, axis=0, keepdims=True) * (1.0 / C)
    centred = values - mean
    var = jnp.sum(centred * centred, axis=0, keepdims=True) * (1.0 / C)
    return centred * lax.rsqrt(var + EPS) * gain + offset


def sigmoid(x):
    return 0.5 * jnp.tanh(0.5 * x) + 0.5


def dot(a, b, dims):
    return lax.dot_general(a, b, (dims, ((), ())), preferred_element_type=F32)


def kernel(
    pair_in, in_gain_in, in_bias_in, projection_in, out_gain_in, out_bias_in, out_weight_in, updated,
    pair, in_gain, in_bias, projection, out_gain, out_bias, out_weight, s0,
    state, normed, gate, cols, wt, wo,
    sa, ra, spread, sx, rx, am, at, bm, tx, ty, tz, tf,
    s1, r1, s2, r2, s3, r3, s4, r4, s5, r5,
):
    loads = [
        pltpu.make_async_copy(src, dst, s0.at[i])
        for i, (src, dst) in enumerate((
            (pair_in, pair), (projection_in, projection), (in_gain_in, in_gain), (in_bias_in, in_bias),
            (out_gain_in, out_gain), (out_bias_in, out_bias), (out_weight_in, out_weight),
        ))
    ]
    for load in loads:
        load.start()

    row = lax.axis_index("row")
    col = lax.axis_index("col")
    core = row % 2
    z = (row // 2) % NZ
    yh = row // (2 * NZ)
    x = col // 2
    y = yh * 2 + col % 2
    p = x * 4 + y

    def zdev(zz):
        return ((yh * NZ + zz) * 2 + core, col)

    def pdev(pp):
        return (((pp % 4 // 2) * NZ + z) * 2 + core, (pp // 4) * 2 + pp % 2)

    sibling = (row - core + (1 - core), col)

    barrier = pltpu.get_barrier_semaphore()

    def greet_z(d, _):
        pl.semaphore_signal(barrier, 1, device_id=zdev((z + d) % NZ), device_id_type=pl.DeviceIdType.MESH)
        return 0

    def across(d):
        return ((x + d // 4) % 4) * 4 + (y + d % 4) % 4

    def greet_p(d, _):
        pl.semaphore_signal(barrier, 1, device_id=pdev(across(d)), device_id_type=pl.DeviceIdType.MESH)
        return 0

    lax.fori_loop(1, NZ, greet_z, 0)
    lax.fori_loop(1, NP, greet_p, 0)
    pl.semaphore_signal(barrier, 1, device_id=sibling, device_id_type=pl.DeviceIdType.MESH)

    def remote(src, dst, send, recv, device):
        return pltpu.make_async_remote_copy(
            src_ref=src, dst_ref=dst, send_sem=send, recv_sem=recv,
            device_id=device, device_id_type=pl.DeviceIdType.MESH,
        )

    low = lax.broadcasted_iota(jnp.int32, (1, 128), 1) < COLS

    def swap(x):
        return pltpu.roll(x, COLS, 1)

    for load in loads:
        load.wait()
    for t in range(8):
        tile = jnp.concatenate([pair[t], pair[t + 8]], axis=0).astype(F32)
        state[:, t * 128:(t + 1) * 128] = tile.T
    for u in range(2):
        for n, ref in enumerate((in_gain, in_bias, out_gain, out_bias)):
            cols[u, n] = jnp.broadcast_to(column(ref[u:u + 1, :]), (C, 128))
        for g in range(5):
            wt[u, g * 128:(g + 1) * 128, :] = projection[u, :, g * 128:(g + 1) * 128].astype(F32).T.astype(BF16)
        wo[u] = out_weight[u].astype(F32).T.astype(BF16)

    for u in range(2):
        def project(t, _):
            lanes = pl.ds(pl.multiple_of(t * 128, 128), 128)
            nrm = norm0(state[:, lanes], cols[u, 0], cols[u, 1]).astype(BF16)
            normed[:, lanes] = nrm
            proj = dot(wt[u, :512, :], nrm, ((1,), (0,)))
            left = (sigmoid(proj[128:256]) * proj[:128]).astype(BF16)
            right = (sigmoid(proj[384:512]) * proj[256:384]).astype(BF16)
            sa[u, :, 0:16, lanes] = left.reshape(NZ, 16, 128)
            sa[u, :, 16:32, lanes] = right.reshape(NZ, 16, 128)
            return 0

        lax.fori_loop(0, 8, project, 0)

        if u == 0:
            pl.semaphore_wait(barrier, NZ - 1 + NP - 1 + 1)
        for d in STEPS[1:]:
            to = (z + d) % NZ
            remote(sa.at[u, to], ra.at[u, z], s1.at[u, d], r1.at[u, z], zdev(to)).start()

        def gates(t, _):
            lanes = pl.ds(pl.multiple_of(t * 128, 128), 128)
            gate[:, lanes] = sigmoid(dot(wt[u, 512:, :], normed[:, lanes], ((1,), (0,))))
            return 0

        lax.fori_loop(0, 8, gates, 0)

        def spread_out(s):
            zs = (z + STEPS[s]) % NZ
            if s > 0:
                remote(sa.at[u, zs], ra.at[u, zs], s1.at[u, 0], r1.at[u, zs], zdev(zs)).wait_recv()
            src = sa.at[u, zs] if s == 0 else ra.at[u, zs]
            for t in range(8):
                vl = src[0:16, t * 128:(t + 1) * 128].astype(F32)
                vr = src[16:32, t * 128:(t + 1) * 128].astype(F32)
                spread[pl.ds(t, 16, stride=16), :] = jnp.where(low, vl, swap(vr))
                spread[pl.ds(8 + t, 16, stride=16), :] = jnp.where(low, swap(vl), vr)
            sx[u, :, s] = spread[...].reshape(NP, 16, 128).astype(BF16)

        def send_plane(g):
            steps = pl.ds(g * GROUP, GROUP)
            rx[u, col, yh, core, steps] = sx[u, p, steps]

            def one(d, _):
                to = across(d)
                remote(sx.at[u, to, steps], rx.at[u, col, yh, core, steps], s2.at[u, g], r2.at[u, g], pdev(to)).start()
                return 0

            [one(d, 0) for d in PLANE]

        def swap_cores(g):
            steps = pl.ds(g * GROUP, GROUP)
            whole = rx.at[u, :, :, core, steps]
            part = sx.at[u, pl.ds(0, NP - 1), steps]
            pltpu.make_async_copy(part, part, r2.at[u, g]).wait()
            remote(whole, whole, s3.at[u, g], r3.at[u, g], sibling).start()

        def build(g):
            steps = pl.ds(g * GROUP, GROUP)
            other = rx.at[u, :, :, 1 - core, steps]
            pltpu.make_async_copy(other, other, r3.at[u, g]).wait()
            for s in range(g * GROUP, (g + 1) * GROUP):
                zs = (z + STEPS[s]) % NZ
                for h in range(2):
                    for k in range(2):
                        place = pl.ds(pl.multiple_of(((h * NZ + zs) * 2 + k) * 16, 16), 16)
                        for c in range(4):
                            x0 = rx[u, 2 * c, h, k, s].astype(F32)
                            x1 = rx[u, 2 * c + 1, h, k, s].astype(F32)
                            am[place, c * 128:(c + 1) * 128] = jnp.where(low, x0, swap(x1)).astype(BF16)
                            bm[place, c * 128:(c + 1) * 128] = jnp.where(low, swap(x0), x1).astype(BF16)

        for g in range(NG):
            for s in range(g * GROUP, (g + 1) * GROUP):
                spread_out(s)
            send_plane(g)
        for g in range(NG):
            swap_cores(g)
        for g in range(NG):
            build(g)

        if u == 1:
            def flip(i, _):
                lanes = pl.ds(pl.multiple_of(i * 128, 128), 128)
                for k in range(4):
                    at[lanes, k * 128:(k + 1) * 128] = am[k * 128:(k + 1) * 128, lanes].astype(F32).T.astype(BF16)
                return 0

            lax.fori_loop(0, 4, flip, 0)
        a_ref = am if u == 0 else at

        def triangle(g):
            rows = []
            for s in BACK[g * GROUP:(g + 1) * GROUP]:
                for h in range(2):
                    r = ((h * NZ + (z + s) % NZ) * 2 + core) * 16
                    rows.append(a_ref[pl.ds(pl.multiple_of(r, 16), 16), :])
            tri = dot(jnp.concatenate(rows, axis=0), bm[...], ((1,), (1 - u,)))
            for h in range(2):
                for c in range(4):
                    first, second = [], []
                    for s in range(GROUP):
                        block = tri[(s * 2 + h) * 16:(s * 2 + h + 1) * 16, c * 128:(c + 1) * 128]
                        first.append(jnp.where(low, block[0:8], swap(block[8:16])))
                        second.append(jnp.where(low, swap(block[0:8]), block[8:16]))
                    tx[u, g, 4 * c + 2 * h] = jnp.concatenate(first, axis=0).astype(BF16)
                    tx[u, g, 4 * c + 2 * h + 1] = jnp.concatenate(second, axis=0).astype(BF16)

        def send_back(g):
            ty[u, g, p] = tx[u, g, p]

            def one(d, _):
                to = across(d)
                remote(tx.at[u, g, to], ty.at[u, g, p], s4.at[u, g], r4.at[u, g], pdev(to)).start()
                return 0

            [one(d, 0) for d in PLANE]

        def gather_back(g):
            part = ty.at[u, g, pl.ds(0, NP - 1)]
            pltpu.make_async_copy(part, part, r4.at[u, g]).wait()
            for h in range(NP):
                spread[pl.ds(h, 16, stride=16), :] = ty[u, g, h].astype(F32)
            for n in range(GROUP):
                d = BACK[g * GROUP + n]
                for t in range(8):
                    at_row = (n * 8 + t) * 16
                    tile = spread[at_row:at_row + 16, :].astype(BF16)
                    if d == 0:
                        tf[u, z, :, t * 128:(t + 1) * 128] = tile
                    else:
                        tz[u, d, :, t * 128:(t + 1) * 128] = tile
                if d:
                    remote(tz.at[u, d], tf.at[u, z], s5.at[u, d], r5.at[u, z], zdev((z + d) % NZ)).start()

        for g in range(NG):
            triangle(g)
            send_back(g)
        for g in range(NG):
            gather_back(g)

        for d in range(1, NZ):
            zs = (z + d) % NZ
            remote(tz.at[u, d], tf.at[u, zs], s5.at[u, d], r5.at[u, zs], zdev(zs)).wait_recv()

        def finish(t, _):
            lanes = pl.ds(pl.multiple_of(t * 128, 128), 128)
            tri = tf[u, :, :, lanes].reshape(H, 128).astype(F32)
            nrm = norm0(tri, cols[u, 2], cols[u, 3]).astype(BF16)
            delta = dot(wo[u], nrm, ((1,), (0,)))
            new = state[:, lanes] + gate[:, lanes] * delta
            if u == 0:
                state[:, lanes] = new.astype(BF16).astype(F32)
            else:
                tile = new.T.astype(BF16)
                updated[t] = tile[0:COLS]
                updated[t + 8] = tile[COLS:]
            return 0

        lax.fori_loop(0, 8, finish, 0)

    for u in range(2):
        for d in range(1, NZ):
            zs = (z + d) % NZ
            remote(sa.at[u, zs], ra.at[u, z], s1.at[u, d], r1.at[u, z], zdev(zs)).wait_send()
            remote(tz.at[u, d], tf.at[u, z], s5.at[u, d], r5.at[u, z], zdev(zs)).wait_send()
        for g in range(NG):
            sent = sx.at[u, pl.ds(0, NP - 1), pl.ds(g * GROUP, GROUP)]
            pltpu.make_async_copy(sent, sent, s2.at[u, g]).wait()
            sent = tx.at[u, g, pl.ds(0, NP - 1)]
            pltpu.make_async_copy(sent, sent, s4.at[u, g]).wait()
            sent = rx.at[u, :, :, core, pl.ds(g * GROUP, GROUP)]
            pltpu.make_async_copy(sent, sent, s3.at[u, g]).wait()


def local(pair, in_gain, in_bias, projection, out_gain, out_bias, out_weight):
    vm = pltpu.VMEM
    dma = pltpu.SemaphoreType.DMA
    return pl.pallas_call(
        kernel,
        out_shape=jax.ShapeDtypeStruct((ROWS, COLS, C), BF16),
        in_specs=[pl.BlockSpec(memory_space=pltpu.HBM)] * 7,
        out_specs=pl.BlockSpec(memory_space=vm),
        scratch_shapes=[
            vm((ROWS, COLS, C), BF16),
            vm((2, C), F32),
            vm((2, C), F32),
            vm((2, C, 640), BF16),
            vm((2, H), F32),
            vm((2, H), F32),
            vm((2, H, C), BF16),
            dma((7,)),
            vm((C, LANES), F32),
            vm((C, LANES), BF16),
            vm((C, LANES), F32),
            vm((2, 4, C, 128), F32),
            vm((2, 640, C), BF16),
            vm((2, C, H), BF16),
            vm((2, NZ, 32, LANES), BF16),
            vm((2, NZ, 32, LANES), BF16),
            vm((256, 128), F32),
            vm((2, NP, NZ, 16, 128), BF16),
            vm((2, 8, 2, 2, NZ, 16, 128), BF16),
            vm((512, 512), BF16),
            vm((512, 512), BF16),
            vm((512, 512), BF16),
            vm((2, NG, NP, 16, 128), BF16),
            vm((2, NG, NP, 16, 128), BF16),
            vm((2, NZ, 16, LANES), BF16),
            vm((2, NZ, 16, LANES), BF16),
            dma((2, NZ)), dma((2, NZ)),
            dma((2, NG)), dma((2, NG)),
            dma((2, NG)), dma((2, NG)),
            dma((2, NG)), dma((2, NG)),
            dma((2, NZ)), dma((2, NZ)),
        ],
        compiler_params=pltpu.CompilerParams(
            collective_id=0, has_side_effects=True, vmem_limit_bytes=62 * 1024 * 1024
        ),
    )(pair, in_gain, in_bias, projection, out_gain, out_bias, out_weight)


def solution(mesh):
    return jax.shard_map(
        local,
        mesh=mesh,
        in_specs=(P("row", "col", None), P(), P(), P(), P(), P(), P()),
        out_specs=P("row", "col", None),
        check_vma=False,
    )
```

```python
import jax
import jax.numpy as jnp
from jax import lax
from jax.experimental import pallas as pl
from jax.experimental.pallas import tpu as pltpu
from jax.sharding import PartitionSpec as P

F32 = jnp.float32
BF16 = jnp.bfloat16
C = 128
H = 128
ROWS = 16
COLS = 64
LANES = ROWS * COLS
NZ = 8
NP = 16
FWD = ((0, 1, 7), (2, 6), (3, 5), (4,))
NF = len(FWD)
SWAP_LAG = 2
GROUP = 2
NG = NZ // GROUP
HALF = LANES // 2
UNROLL = 4
STEPS = sum(FWD, ())
START = tuple(sum(len(f) for f in FWD[:g]) for g in range(NF + 1))


def part(g):
    return pl.ds(START[g], len(FWD[g]))


PLANE = (10, 6, 9, 11, 14, 2, 8, 5, 7, 13, 15, 1, 3, 4, 12)
BACK = (3, 5, 4, 2, 6, 1, 7, 0)
EPS = 1e-05


def column(row):
    eye = lax.broadcasted_iota(jnp.int32, (C, C), 0) == lax.broadcasted_iota(jnp.int32, (C, C), 1)
    return jnp.sum(jnp.where(eye, jnp.broadcast_to(row, (C, C)), 0.0), axis=1, keepdims=True)


def norm0(values, gain, offset):
    mean = jnp.sum(values, axis=0, keepdims=True) * (1.0 / C)
    centred = values - mean
    var = jnp.sum(centred * centred, axis=0, keepdims=True) * (1.0 / C)
    return centred * lax.rsqrt(var + EPS) * gain + offset


def sigmoid(x):
    return 0.5 * jnp.tanh(0.5 * x) + 0.5


def dot(a, b, dims):
    return lax.dot_general(a, b, (dims, ((), ())), preferred_element_type=F32)


def kernel(
    pair_in, in_gain_in, in_bias_in, projection_in, out_gain_in, out_bias_in, out_weight_in, updated,
    pair, in_gain, in_bias, projection, out_gain, out_bias, out_weight, s0,
    state, normed, gate, cols, wt, wo,
    sa, ra, spread, sx, rx, am, at, bm, ts, tx, ty, spread2, tz, tf,
    s1, r1, s2, r2, s3, r3, s4, r4, s5, r5,
):
    loads = [
        pltpu.make_async_copy(src, dst, s0.at[i])
        for i, (src, dst) in enumerate((
            (pair_in, pair), (projection_in, projection), (in_gain_in, in_gain), (in_bias_in, in_bias),
            (out_gain_in, out_gain), (out_bias_in, out_bias), (out_weight_in, out_weight),
        ))
    ]
    for load in loads:
        load.start()

    row = lax.axis_index("row")
    col = lax.axis_index("col")
    core = row % 2
    z = (row // 2) % NZ
    yh = row // (2 * NZ)
    x = col // 2
    y = yh * 2 + col % 2
    p = x * 4 + y

    def zdev(zz):
        return ((yh * NZ + zz) * 2 + core, col)

    def pdev(pp):
        return (((pp % 4 // 2) * NZ + z) * 2 + core, (pp // 4) * 2 + pp % 2)

    sibling = (row - core + (1 - core), col)

    barrier = pltpu.get_barrier_semaphore()

    def greet_z(d, _):
        pl.semaphore_signal(barrier, 1, device_id=zdev((z + d) % NZ), device_id_type=pl.DeviceIdType.MESH)
        return 0

    def across(d):
        return ((x + d // 4) % 4) * 4 + (y + d % 4) % 4

    def greet_p(d, _):
        pl.semaphore_signal(barrier, 1, device_id=pdev(across(d)), device_id_type=pl.DeviceIdType.MESH)
        return 0

    lax.fori_loop(1, NZ, greet_z, 0)
    lax.fori_loop(1, NP, greet_p, 0)
    pl.semaphore_signal(barrier, 1, device_id=sibling, device_id_type=pl.DeviceIdType.MESH)

    def remote(src, dst, send, recv, device):
        return pltpu.make_async_remote_copy(
            src_ref=src, dst_ref=dst, send_sem=send, recv_sem=recv,
            device_id=device, device_id_type=pl.DeviceIdType.MESH,
        )

    low = lax.broadcasted_iota(jnp.int32, (1, 128), 1) < COLS

    def swap(x):
        return pltpu.roll(x, COLS, 1)

    for load in loads:
        load.wait()
    for t in range(8):
        tile = jnp.concatenate([pair[t], pair[t + 8]], axis=0).astype(F32)
        state[:, t * 128:(t + 1) * 128] = tile.T
    for u in range(2):
        for n, ref in enumerate((in_gain, in_bias, out_gain, out_bias)):
            cols[u, n] = jnp.broadcast_to(column(ref[u:u + 1, :]), (C, 128))
        for g in range(5):
            wt[u, g * 128:(g + 1) * 128, :] = projection[u, :, g * 128:(g + 1) * 128].astype(F32).T.astype(BF16)
        wo[u] = out_weight[u].astype(F32).T.astype(BF16)

    def project(u, half):
        def one(t, _):
            lanes = pl.ds(pl.multiple_of((half * 4 + t) * 128, 128), 128)
            part_lanes = pl.ds(pl.multiple_of(t * 128, 128), 128)
            nrm = norm0(state[:, lanes], cols[u, 0], cols[u, 1]).astype(BF16)
            normed[:, lanes] = nrm
            proj = dot(wt[u, :512, :], nrm, ((1,), (0,)))
            left = (sigmoid(proj[128:256]) * proj[:128]).astype(BF16)
            right = (sigmoid(proj[384:512]) * proj[256:384]).astype(BF16)
            sa[u, half, :, 0:16, part_lanes] = left.reshape(NZ, 16, 128)
            sa[u, half, :, 16:32, part_lanes] = right.reshape(NZ, 16, 128)
            return 0

        lax.fori_loop(0, 4, one, 0, unroll=UNROLL)

    def send_z(u, half):
        for d in STEPS[1:]:
            to = (z + d) % NZ
            remote(sa.at[u, half, to], ra.at[u, half, z], s1.at[u, half, d], r1.at[u, half, z], zdev(to)).start()

    project(0, 0)
    pl.semaphore_wait(barrier, NZ - 1 + NP - 1 + 1)
    send_z(0, 0)
    project(0, 1)
    send_z(0, 1)

    for u in range(2):
        def gates(t, _):
            lanes = pl.ds(pl.multiple_of(t * 128, 128), 128)
            gate[:, lanes] = sigmoid(dot(wt[u, 512:, :], normed[:, lanes], ((1,), (0,))))
            return 0

        lax.fori_loop(0, 8, gates, 0, unroll=UNROLL)

        def spread_out(s):
            zs = (z + STEPS[s]) % NZ
            for half in range(2):
                if s > 0:
                    remote(sa.at[u, half, zs], ra.at[u, half, zs], s1.at[u, half, 0], r1.at[u, half, zs], zdev(zs)).wait_recv()
                src = sa.at[u, half, zs] if s == 0 else ra.at[u, half, zs]
                for t in range(4):
                    vl = src[0:16, t * 128:(t + 1) * 128].astype(F32)
                    vr = src[16:32, t * 128:(t + 1) * 128].astype(F32)
                    n = half * 4 + t
                    spread[pl.ds(n, 16, stride=16), :] = jnp.where(low, vl, swap(vr))
                    spread[pl.ds(8 + n, 16, stride=16), :] = jnp.where(low, swap(vl), vr)
            sx[u, :, s] = spread[...].reshape(NP, 16, 128).astype(BF16)

        def send_plane(g):
            steps = part(g)
            rx[u, col, yh, core, steps] = sx[u, p, steps]

            def one(d, _):
                to = across(d)
                remote(sx.at[u, to, steps], rx.at[u, col, yh, core, steps], s2.at[u, g], r2.at[u, g], pdev(to)).start()
                return 0

            [one(d, 0) for d in PLANE]

        def swap_cores(g):
            steps = part(g)
            whole = rx.at[u, :, :, core, steps]
            most = sx.at[u, pl.ds(0, NP - 1), steps]
            pltpu.make_async_copy(most, most, r2.at[u, g]).wait()
            remote(whole, whole, s3.at[u, g], r3.at[u, g], sibling).start()

        def build(g):
            steps = part(g)
            other = rx.at[u, :, :, 1 - core, steps]
            pltpu.make_async_copy(other, other, r3.at[u, g]).wait()
            for s in range(START[g], START[g + 1]):
                zs = (z + STEPS[s]) % NZ
                for h in range(2):
                    for k in range(2):
                        place = pl.ds(pl.multiple_of(((h * NZ + zs) * 2 + k) * 16, 16), 16)
                        for c in range(4):
                            x0 = rx[u, 2 * c, h, k, s].astype(F32)
                            x1 = rx[u, 2 * c + 1, h, k, s].astype(F32)
                            am[place, c * 128:(c + 1) * 128] = jnp.where(low, x0, swap(x1)).astype(BF16)
                            bm[place, c * 128:(c + 1) * 128] = jnp.where(low, swap(x0), x1).astype(BF16)

        for g in range(NF):
            for s in range(START[g], START[g + 1]):
                spread_out(s)
            send_plane(g)
            if g >= SWAP_LAG:
                swap_cores(g - SWAP_LAG)
        for g in range(max(0, NF - SWAP_LAG), NF):
            swap_cores(g)
        for g in range(NF):
            build(g)

        if u == 1:
            def flip(i, _):
                lanes = pl.ds(pl.multiple_of(i * 128, 128), 128)
                for k in range(4):
                    at[lanes, k * 128:(k + 1) * 128] = am[k * 128:(k + 1) * 128, lanes].astype(F32).T.astype(BF16)
                return 0

            lax.fori_loop(0, 4, flip, 0)
        a_ref = am if u == 0 else at

        def triangle(g):
            rows = []
            for s in BACK[g * GROUP:(g + 1) * GROUP]:
                for h in range(2):
                    r = ((h * NZ + (z + s) % NZ) * 2 + core) * 16
                    rows.append(a_ref[pl.ds(pl.multiple_of(r, 16), 16), :])
            tri = dot(jnp.concatenate(rows, axis=0), bm[...], ((1,), (1 - u,)))
            for n in range(GROUP):
                for h in range(2):
                    for c in range(4):
                        block = tri[(n * 2 + h) * 16:(n * 2 + h + 1) * 16, c * 128:(c + 1) * 128]
                        first = jnp.where(low, block[0:8], swap(block[8:16]))
                        second = jnp.where(low, swap(block[0:8]), block[8:16])
                        at_row = (g * GROUP + n) * 4
                        for half in range(2):
                            rows4 = slice(half * 4, half * 4 + 4)
                            ts[half, 4 * c + 2 * h, at_row:at_row + 4] = first[rows4]
                            ts[half, 4 * c + 2 * h + 1, at_row:at_row + 4] = second[rows4]

        def send_back(half):
            tx[u, half] = ts[half].astype(BF16)
            for d in PLANE:
                to = across(d)
                remote(tx.at[u, half, to], ty.at[u, half, p], s4.at[u, half], r4.at[u, half], pdev(to)).start()
            ty[u, half, p] = tx[u, half, p]

        def gather_back(half):
            most = ty.at[u, half, pl.ds(0, NP - 1)]
            pltpu.make_async_copy(most, most, r4.at[u, half]).wait()
            for h in range(NP):
                spread2[pl.ds(h, 32, stride=16), :] = ty[u, half, h].astype(F32)
            for n in range(NZ):
                d = BACK[n]
                for t in range(4):
                    at_row = (n * 4 + t) * 16
                    tile = spread2[at_row:at_row + 16, :].astype(BF16)
                    if d == 0:
                        tf[u, half, z, :, t * 128:(t + 1) * 128] = tile
                    else:
                        tz[u, half, d, :, t * 128:(t + 1) * 128] = tile
                if d:
                    remote(tz.at[u, half, d], tf.at[u, half, z], s5.at[u, half, d], r5.at[u, half, z], zdev((z + d) % NZ)).start()

        def wait_back(half):
            for d in range(1, NZ):
                zs = (z + d) % NZ
                remote(tz.at[u, half, d], tf.at[u, half, zs], s5.at[u, half, d], r5.at[u, half, zs], zdev(zs)).wait_recv()

        def finish(half):
            def one(t, _):
                lanes = pl.ds(pl.multiple_of((half * 4 + t) * 128, 128), 128)
                tri = tf[u, half, :, :, pl.ds(pl.multiple_of(t * 128, 128), 128)].reshape(H, 128).astype(F32)
                nrm = norm0(tri, cols[u, 2], cols[u, 3]).astype(BF16)
                delta = dot(wo[u], nrm, ((1,), (0,)))
                new = state[:, lanes] + gate[:, lanes] * delta
                if u == 0:
                    state[:, lanes] = new.astype(BF16).astype(F32)
                else:
                    tile = new.T.astype(BF16)
                    updated[half * 4 + t] = tile[0:COLS]
                    updated[half * 4 + t + 8] = tile[COLS:]
                return 0

            lax.fori_loop(0, 4, one, 0, unroll=UNROLL)

        for g in range(NG):
            triangle(g)
        for half in range(2):
            send_back(half)
        for half in range(2):
            gather_back(half)
        for half in range(2):
            wait_back(half)
            finish(half)
            if u == 0:
                project(1, half)
                send_z(1, half)

    for u in range(2):
        for half in range(2):
            for d in range(1, NZ):
                zs = (z + d) % NZ
                remote(sa.at[u, half, zs], ra.at[u, half, z], s1.at[u, half, d], r1.at[u, half, z], zdev(zs)).wait_send()
                remote(tz.at[u, half, d], tf.at[u, half, z], s5.at[u, half, d], r5.at[u, half, z], zdev(zs)).wait_send()
            sent = tx.at[u, half, pl.ds(0, NP - 1)]
            pltpu.make_async_copy(sent, sent, s4.at[u, half]).wait()
        for g in range(NF):
            sent = sx.at[u, pl.ds(0, NP - 1), part(g)]
            pltpu.make_async_copy(sent, sent, s2.at[u, g]).wait()
            sent = rx.at[u, :, :, core, part(g)]
            pltpu.make_async_copy(sent, sent, s3.at[u, g]).wait()


def local(pair, in_gain, in_bias, projection, out_gain, out_bias, out_weight):
    vm = pltpu.VMEM
    dma = pltpu.SemaphoreType.DMA
    return pl.pallas_call(
        kernel,
        out_shape=jax.ShapeDtypeStruct((ROWS, COLS, C), BF16),
        in_specs=[pl.BlockSpec(memory_space=pltpu.HBM)] * 7,
        out_specs=pl.BlockSpec(memory_space=vm),
        scratch_shapes=[
            vm((ROWS, COLS, C), BF16),
            vm((2, C), F32),
            vm((2, C), F32),
            vm((2, C, 640), BF16),
            vm((2, H), F32),
            vm((2, H), F32),
            vm((2, H, C), BF16),
            dma((7,)),
            vm((C, LANES), F32),
            vm((C, LANES), BF16),
            vm((C, LANES), F32),
            vm((2, 4, C, 128), F32),
            vm((2, 640, C), BF16),
            vm((2, C, H), BF16),
            vm((2, 2, NZ, 32, HALF), BF16),
            vm((2, 2, NZ, 32, HALF), BF16),
            vm((256, 128), F32),
            vm((2, NP, NZ, 16, 128), BF16),
            vm((2, 8, 2, 2, NZ, 16, 128), BF16),
            vm((512, 512), BF16),
            vm((512, 512), BF16),
            vm((512, 512), BF16),
            vm((2, NP, 32, 128), F32),
            vm((2, 2, NP, 32, 128), BF16),
            vm((2, 2, NP, 32, 128), BF16),
            vm((512, 128), F32),
            vm((2, 2, NZ, 16, HALF), BF16),
            vm((2, 2, NZ, 16, HALF), BF16),
            dma((2, 2, NZ)), dma((2, 2, NZ)),
            dma((2, NF)), dma((2, NF)),
            dma((2, NF)), dma((2, NF)),
            dma((2, 2)), dma((2, 2)),
            dma((2, 2, NZ)), dma((2, 2, NZ)),
        ],
        compiler_params=pltpu.CompilerParams(
            collective_id=0, has_side_effects=True, vmem_limit_bytes=62 * 1024 * 1024
        ),
    )(pair, in_gain, in_bias, projection, out_gain, out_bias, out_weight)


def solution(mesh):
    return jax.shard_map(
        local,
        mesh=mesh,
        in_specs=(P("row", "col", None), P(), P(), P(), P(), P(), P()),
        out_specs=P("row", "col", None),
        check_vma=False,
    )
```

```python
import jax
import jax.numpy as jnp
from jax import lax
from jax.experimental import pallas as pl
from jax.experimental.pallas import tpu as pltpu
from jax.sharding import PartitionSpec as P

F32 = jnp.float32
BF16 = jnp.bfloat16
C = 128
H = 128
ROWS = 16
COLS = 64
LANES = ROWS * COLS
NZ = 8
NP = 16
FWD = ((0, 1, 7), (2, 6), (3, 5), (4,))
NF = len(FWD)
SWAP_LAG = 3
GROUP = 2
NG = NZ // GROUP
HALF = LANES // 2
UNROLL = 4
STEPS = sum(FWD, ())
START = tuple(sum(len(f) for f in FWD[:g]) for g in range(NF + 1))


def part(g):
    return pl.ds(START[g], len(FWD[g]))


PLANE = (10, 6, 9, 11, 14, 2, 8, 5, 7, 13, 15, 1, 3, 4, 12)
BACK = (3, 5, 4, 2, 6, 1, 7, 0)
EPS = 1e-05


def column(row):
    eye = lax.broadcasted_iota(jnp.int32, (C, C), 0) == lax.broadcasted_iota(jnp.int32, (C, C), 1)
    return jnp.sum(jnp.where(eye, jnp.broadcast_to(row, (C, C)), 0.0), axis=1, keepdims=True)


def norm0(values, gain, offset):
    mean = jnp.sum(values, axis=0, keepdims=True) * (1.0 / C)
    centred = values - mean
    var = jnp.sum(centred * centred, axis=0, keepdims=True) * (1.0 / C)
    return centred * lax.rsqrt(var + EPS) * gain + offset


def sigmoid(x):
    return 0.5 * jnp.tanh(0.5 * x) + 0.5


def dot(a, b, dims):
    return lax.dot_general(a, b, (dims, ((), ())), preferred_element_type=F32)


def kernel(
    pair_in, in_gain_in, in_bias_in, projection_in, out_gain_in, out_bias_in, out_weight_in, updated,
    pair, in_gain, in_bias, projection, out_gain, out_bias, out_weight, s0,
    state, normed, gate, cols, wt, wo,
    sa, ra, spread, sx, rx, am, at, bm, ts, tx, ty, spread2, tz, tf,
    s1, r1, s2, r2, s3, r3, s4, r4, s5, r5,
):
    loads = [
        pltpu.make_async_copy(src, dst, s0.at[i])
        for i, (src, dst) in enumerate((
            (pair_in, pair), (projection_in, projection), (in_gain_in, in_gain), (in_bias_in, in_bias),
            (out_gain_in, out_gain), (out_bias_in, out_bias), (out_weight_in, out_weight),
        ))
    ]
    for load in loads:
        load.start()

    row = lax.axis_index("row")
    col = lax.axis_index("col")
    core = row % 2
    z = (row // 2) % NZ
    yh = row // (2 * NZ)
    x = col // 2
    y = yh * 2 + col % 2
    p = x * 4 + y

    def zdev(zz):
        return ((yh * NZ + zz) * 2 + core, col)

    def pdev(pp):
        return (((pp % 4 // 2) * NZ + z) * 2 + core, (pp // 4) * 2 + pp % 2)

    def twin(pp):
        return (((pp % 4 // 2) * NZ + z) * 2 + (1 - core), (pp // 4) * 2 + pp % 2)

    sibling = (row - core + (1 - core), col)

    barrier = pltpu.get_barrier_semaphore()

    def greet_z(d, _):
        pl.semaphore_signal(barrier, 1, device_id=zdev((z + d) % NZ), device_id_type=pl.DeviceIdType.MESH)
        return 0

    def across(d):
        return ((x + d // 4) % 4) * 4 + (y + d % 4) % 4

    def greet_p(d, _):
        pl.semaphore_signal(barrier, 1, device_id=pdev(across(d)), device_id_type=pl.DeviceIdType.MESH)
        pl.semaphore_signal(barrier, 1, device_id=twin(across(d)), device_id_type=pl.DeviceIdType.MESH)
        return 0

    lax.fori_loop(1, NZ, greet_z, 0)
    lax.fori_loop(1, NP, greet_p, 0)
    pl.semaphore_signal(barrier, 1, device_id=sibling, device_id_type=pl.DeviceIdType.MESH)

    def remote(src, dst, send, recv, device):
        return pltpu.make_async_remote_copy(
            src_ref=src, dst_ref=dst, send_sem=send, recv_sem=recv,
            device_id=device, device_id_type=pl.DeviceIdType.MESH,
        )

    low = lax.broadcasted_iota(jnp.int32, (1, 128), 1) < COLS

    def swap(x):
        return pltpu.roll(x, COLS, 1)

    for load in loads:
        load.wait()
    for t in range(8):
        tile = jnp.concatenate([pair[t], pair[t + 8]], axis=0).astype(F32)
        state[:, t * 128:(t + 1) * 128] = tile.T
    for u in range(2):
        for n, ref in enumerate((in_gain, in_bias, out_gain, out_bias)):
            cols[u, n] = jnp.broadcast_to(column(ref[u:u + 1, :]), (C, 128))
        for g in range(5):
            wt[u, g * 128:(g + 1) * 128, :] = projection[u, :, g * 128:(g + 1) * 128].astype(F32).T.astype(BF16)
        wo[u] = out_weight[u].astype(F32).T.astype(BF16)

    def project(u, half):
        def one(t, _):
            lanes = pl.ds(pl.multiple_of((half * 4 + t) * 128, 128), 128)
            part_lanes = pl.ds(pl.multiple_of(t * 128, 128), 128)
            nrm = norm0(state[:, lanes], cols[u, 0], cols[u, 1]).astype(BF16)
            normed[:, lanes] = nrm
            proj = dot(wt[u, :512, :], nrm, ((1,), (0,)))
            left = (sigmoid(proj[128:256]) * proj[:128]).astype(BF16)
            right = (sigmoid(proj[384:512]) * proj[256:384]).astype(BF16)
            sa[u, half, :, 0:16, part_lanes] = left.reshape(NZ, 16, 128)
            sa[u, half, :, 16:32, part_lanes] = right.reshape(NZ, 16, 128)
            return 0

        lax.fori_loop(0, 4, one, 0, unroll=UNROLL)

    def send_z(u, half):
        for d in STEPS[1:]:
            to = (z + d) % NZ
            remote(sa.at[u, half, to], ra.at[u, half, z], s1.at[u, half, d], r1.at[u, half, z], zdev(to)).start()

    project(0, 0)
    pl.semaphore_wait(barrier, NZ - 1 + 2 * (NP - 1) + 1)
    send_z(0, 0)
    project(0, 1)
    send_z(0, 1)

    for u in range(2):
        def gates(t, _):
            lanes = pl.ds(pl.multiple_of(t * 128, 128), 128)
            gate[:, lanes] = sigmoid(dot(wt[u, 512:, :], normed[:, lanes], ((1,), (0,))))
            return 0

        lax.fori_loop(0, 8, gates, 0, unroll=UNROLL)

        def spread_out(s):
            zs = (z + STEPS[s]) % NZ
            for half in range(2):
                if s > 0:
                    remote(sa.at[u, half, zs], ra.at[u, half, zs], s1.at[u, half, 0], r1.at[u, half, zs], zdev(zs)).wait_recv()
                src = sa.at[u, half, zs] if s == 0 else ra.at[u, half, zs]
                for t in range(4):
                    vl = src[0:16, t * 128:(t + 1) * 128].astype(F32)
                    vr = src[16:32, t * 128:(t + 1) * 128].astype(F32)
                    n = half * 4 + t
                    spread[pl.ds(n, 16, stride=16), :] = jnp.where(low, vl, swap(vr))
                    spread[pl.ds(8 + n, 16, stride=16), :] = jnp.where(low, swap(vl), vr)
            sx[u, :, s] = spread[...].reshape(NP, 16, 128).astype(BF16)

        def send_plane(g):
            steps = part(g)
            here = (u, col, yh, core, steps)
            for d in PLANE:
                to = across(d)
                if g == NF - 1:
                    remote(sx.at[u, to, steps], rx.at[here], s3.at[u, g], r3.at[u, g], twin(to)).start()
                remote(sx.at[u, to, steps], rx.at[here], s2.at[u, g], r2.at[u, g], pdev(to)).start()
            if g == NF - 1:
                remote(sx.at[u, p, steps], rx.at[here], s3.at[u, g], r3.at[u, g], sibling).start()
            rx[u, col, yh, core, steps] = sx[u, p, steps]

        def swap_cores(g):
            steps = part(g)
            whole = rx.at[u, :, :, core, steps]
            most = sx.at[u, pl.ds(0, NP - 1), steps]
            pltpu.make_async_copy(most, most, r2.at[u, g]).wait()
            if g < NF - 1:
                remote(whole, whole, s3.at[u, g], r3.at[u, g], sibling).start()

        def build(g):
            steps = part(g)
            other = rx.at[u, :, :, 1 - core, steps]
            pltpu.make_async_copy(other, other, r3.at[u, g]).wait()
            for s in range(START[g], START[g + 1]):
                zs = (z + STEPS[s]) % NZ
                for h in range(2):
                    for k in range(2):
                        place = pl.ds(pl.multiple_of(((h * NZ + zs) * 2 + k) * 16, 16), 16)
                        for c in range(4):
                            x0 = rx[u, 2 * c, h, k, s].astype(F32)
                            x1 = rx[u, 2 * c + 1, h, k, s].astype(F32)
                            am[place, c * 128:(c + 1) * 128] = jnp.where(low, x0, swap(x1)).astype(BF16)
                            bm[place, c * 128:(c + 1) * 128] = jnp.where(low, swap(x0), x1).astype(BF16)

        for g in range(NF):
            for s in range(START[g], START[g + 1]):
                spread_out(s)
            send_plane(g)
            if g >= SWAP_LAG:
                swap_cores(g - SWAP_LAG)
        for g in range(max(0, NF - SWAP_LAG), NF - 1):
            swap_cores(g)
        swap_cores(NF - 1)
        for g in range(NF):
            build(g)

        if u == 1:
            def flip(i, _):
                lanes = pl.ds(pl.multiple_of(i * 128, 128), 128)
                for k in range(4):
                    at[lanes, k * 128:(k + 1) * 128] = am[k * 128:(k + 1) * 128, lanes].astype(F32).T.astype(BF16)
                return 0

            lax.fori_loop(0, 4, flip, 0)
        a_ref = am if u == 0 else at

        def triangle(g):
            rows = []
            for s in BACK[g * GROUP:(g + 1) * GROUP]:
                for h in range(2):
                    r = ((h * NZ + (z + s) % NZ) * 2 + core) * 16
                    rows.append(a_ref[pl.ds(pl.multiple_of(r, 16), 16), :])
            tri = dot(jnp.concatenate(rows, axis=0), bm[...], ((1,), (1 - u,)))
            for n in range(GROUP):
                for h in range(2):
                    for c in range(4):
                        block = tri[(n * 2 + h) * 16:(n * 2 + h + 1) * 16, c * 128:(c + 1) * 128]
                        first = jnp.where(low, block[0:8], swap(block[8:16]))
                        second = jnp.where(low, swap(block[0:8]), block[8:16])
                        at_row = (g * GROUP + n) * 4
                        for half in range(2):
                            rows4 = slice(half * 4, half * 4 + 4)
                            ts[half, 4 * c + 2 * h, at_row:at_row + 4] = first[rows4]
                            ts[half, 4 * c + 2 * h + 1, at_row:at_row + 4] = second[rows4]

        def send_back(half):
            tx[u, half] = ts[half].astype(BF16)
            for d in PLANE:
                to = across(d)
                remote(tx.at[u, half, to], ty.at[u, half, p], s4.at[u, half], r4.at[u, half], pdev(to)).start()
            ty[u, half, p] = tx[u, half, p]

        def gather_back(half):
            most = ty.at[u, half, pl.ds(0, NP - 1)]
            pltpu.make_async_copy(most, most, r4.at[u, half]).wait()
            for h in range(NP):
                spread2[pl.ds(h, 32, stride=16), :] = ty[u, half, h].astype(F32)
            for n in range(NZ):
                d = BACK[n]
                for t in range(4):
                    at_row = (n * 4 + t) * 16
                    tile = spread2[at_row:at_row + 16, :].astype(BF16)
                    if d == 0:
                        tf[u, half, z, :, t * 128:(t + 1) * 128] = tile
                    else:
                        tz[u, half, d, :, t * 128:(t + 1) * 128] = tile
                if d:
                    remote(tz.at[u, half, d], tf.at[u, half, z], s5.at[u, half, d], r5.at[u, half, z], zdev((z + d) % NZ)).start()

        def wait_back(half):
            for d in range(1, NZ):
                zs = (z + d) % NZ
                remote(tz.at[u, half, d], tf.at[u, half, zs], s5.at[u, half, d], r5.at[u, half, zs], zdev(zs)).wait_recv()

        def finish(half):
            def one(t, _):
                lanes = pl.ds(pl.multiple_of((half * 4 + t) * 128, 128), 128)
                tri = tf[u, half, :, :, pl.ds(pl.multiple_of(t * 128, 128), 128)].reshape(H, 128).astype(F32)
                nrm = norm0(tri, cols[u, 2], cols[u, 3]).astype(BF16)
                delta = dot(wo[u], nrm, ((1,), (0,)))
                new = state[:, lanes] + gate[:, lanes] * delta
                if u == 0:
                    state[:, lanes] = new.astype(BF16).astype(F32)
                else:
                    tile = new.T.astype(BF16)
                    updated[half * 4 + t] = tile[0:COLS]
                    updated[half * 4 + t + 8] = tile[COLS:]
                return 0

            lax.fori_loop(0, 4, one, 0, unroll=UNROLL)

        for g in range(NG):
            triangle(g)
        for half in range(2):
            send_back(half)
        for half in range(2):
            gather_back(half)
        for half in range(2):
            wait_back(half)
            finish(half)
            if u == 0:
                project(1, half)
                send_z(1, half)

    for u in range(2):
        for half in range(2):
            for d in range(1, NZ):
                zs = (z + d) % NZ
                remote(sa.at[u, half, zs], ra.at[u, half, z], s1.at[u, half, d], r1.at[u, half, z], zdev(zs)).wait_send()
                remote(tz.at[u, half, d], tf.at[u, half, z], s5.at[u, half, d], r5.at[u, half, z], zdev(zs)).wait_send()
            sent = tx.at[u, half, pl.ds(0, NP - 1)]
            pltpu.make_async_copy(sent, sent, s4.at[u, half]).wait()
        for g in range(NF):
            sent = sx.at[u, pl.ds(0, NP - 1), part(g)]
            pltpu.make_async_copy(sent, sent, s2.at[u, g]).wait()
            sent = sx.at[u, :, part(g)] if g == NF - 1 else rx.at[u, :, :, core, part(g)]
            pltpu.make_async_copy(sent, sent, s3.at[u, g]).wait()


def local(pair, in_gain, in_bias, projection, out_gain, out_bias, out_weight):
    vm = pltpu.VMEM
    dma = pltpu.SemaphoreType.DMA
    return pl.pallas_call(
        kernel,
        out_shape=jax.ShapeDtypeStruct((ROWS, COLS, C), BF16),
        in_specs=[pl.BlockSpec(memory_space=pltpu.HBM)] * 7,
        out_specs=pl.BlockSpec(memory_space=vm),
        scratch_shapes=[
            vm((ROWS, COLS, C), BF16),
            vm((2, C), F32),
            vm((2, C), F32),
            vm((2, C, 640), BF16),
            vm((2, H), F32),
            vm((2, H), F32),
            vm((2, H, C), BF16),
            dma((7,)),
            vm((C, LANES), F32),
            vm((C, LANES), BF16),
            vm((C, LANES), F32),
            vm((2, 4, C, 128), F32),
            vm((2, 640, C), BF16),
            vm((2, C, H), BF16),
            vm((2, 2, NZ, 32, HALF), BF16),
            vm((2, 2, NZ, 32, HALF), BF16),
            vm((256, 128), F32),
            vm((2, NP, NZ, 16, 128), BF16),
            vm((2, 8, 2, 2, NZ, 16, 128), BF16),
            vm((512, 512), BF16),
            vm((512, 512), BF16),
            vm((512, 512), BF16),
            vm((2, NP, 32, 128), F32),
            vm((2, 2, NP, 32, 128), BF16),
            vm((2, 2, NP, 32, 128), BF16),
            vm((512, 128), F32),
            vm((2, 2, NZ, 16, HALF), BF16),
            vm((2, 2, NZ, 16, HALF), BF16),
            dma((2, 2, NZ)), dma((2, 2, NZ)),
            dma((2, NF)), dma((2, NF)),
            dma((2, NF)), dma((2, NF)),
            dma((2, 2)), dma((2, 2)),
            dma((2, 2, NZ)), dma((2, 2, NZ)),
        ],
        compiler_params=pltpu.CompilerParams(
            collective_id=0, has_side_effects=True, vmem_limit_bytes=62 * 1024 * 1024
        ),
    )(pair, in_gain, in_bias, projection, out_gain, out_bias, out_weight)


def solution(mesh):
    return jax.shard_map(
        local,
        mesh=mesh,
        in_specs=(P("row", "col", None), P(), P(), P(), P(), P(), P()),
        out_specs=P("row", "col", None),
        check_vma=False,
    )
```

```python
import jax
import jax.numpy as jnp
from jax import lax
from jax.experimental import pallas as pl
from jax.experimental.pallas import tpu as pltpu
from jax.sharding import PartitionSpec as P

F32 = jnp.float32
BF16 = jnp.bfloat16
C = 128
H = 128
ROWS = 16
COLS = 64
LANES = ROWS * COLS
NZ = 8
NP = 16
FWD = ((0, 1, 7), (2, 6), (3, 5), (4,))
NF = len(FWD)
SWAP_LAG = 3
GROUP = 2
NG = NZ // GROUP
HALF = LANES // 2
UNROLL = 4
STEPS = sum(FWD, ())
START = tuple(sum(len(f) for f in FWD[:g]) for g in range(NF + 1))


def part(g):
    return pl.ds(START[g], len(FWD[g]))


PLANE = (10, 6, 9, 11, 14, 2, 8, 5, 7, 13, 15, 1, 3, 4, 12)
BACK = (3, 5, 4, 2, 6, 1, 7, 0)
EPS = 1e-05


def column(row):
    eye = lax.broadcasted_iota(jnp.int32, (C, C), 0) == lax.broadcasted_iota(jnp.int32, (C, C), 1)
    return jnp.sum(jnp.where(eye, jnp.broadcast_to(row, (C, C)), 0.0), axis=1, keepdims=True)


def norm0(values, gain, offset):
    mean = jnp.sum(values, axis=0, keepdims=True) * (1.0 / C)
    centred = values - mean
    var = jnp.sum(centred * centred, axis=0, keepdims=True) * (1.0 / C)
    return centred * lax.rsqrt(var + EPS) * gain + offset


def sigmoid(x):
    return 0.5 * jnp.tanh(0.5 * x) + 0.5


def dot(a, b, dims):
    return lax.dot_general(a, b, (dims, ((), ())), preferred_element_type=F32)


def kernel(
    pair_in, in_gain_in, in_bias_in, projection_in, out_gain_in, out_bias_in, out_weight_in, updated,
    pair, in_gain, in_bias, projection, out_gain, out_bias, out_weight, s0,
    state, normed, gate, cols, wt, wo,
    sa, ra, spread, sx, rx, am, at, bm, ts, tx, ty, spread2, tz, tf,
    s1, r1, s2, r2, s3, r3, s4, r4, s5, r5,
):
    loads = [
        pltpu.make_async_copy(src, dst, s0.at[i])
        for i, (src, dst) in enumerate((
            (pair_in, pair), (projection_in, projection), (in_gain_in, in_gain), (in_bias_in, in_bias),
            (out_gain_in, out_gain), (out_bias_in, out_bias), (out_weight_in, out_weight),
        ))
    ]
    for load in loads:
        load.start()

    row = lax.axis_index("row")
    col = lax.axis_index("col")
    core = lax.rem(row, 2)
    z = lax.rem(lax.div(row, 2), NZ)
    yh = lax.div(row, 2 * NZ)
    x = lax.div(col, 2)
    y = yh * 2 + lax.rem(col, 2)
    p = x * 4 + y
    other = 1 - core
    ring_z = [z] + [lax.rem(z + d, NZ) for d in range(1, NZ)]
    ring_x = [x] + [lax.rem(x + d, 4) for d in range(1, 4)]
    ring_y = [y] + [lax.rem(y + d, 4) for d in range(1, 4)]
    row_y = [(lax.div(v, 2) * NZ + z) * 2 for v in ring_y]
    col_y = [lax.rem(v, 2) for v in ring_y]
    yh_row = yh * (2 * NZ) + core

    def zdev(d):
        return (ring_z[d] * 2 + yh_row, col)

    def across(d):
        return ring_x[d // 4] * 4 + ring_y[d % 4]

    def pdev(d):
        return (row_y[d % 4] + core, ring_x[d // 4] * 2 + col_y[d % 4])

    def twin(d):
        return (row_y[d % 4] + other, ring_x[d // 4] * 2 + col_y[d % 4])

    sibling = (row - core + other, col)

    barrier = pltpu.get_barrier_semaphore()

    def greet(device):
        pl.semaphore_signal(barrier, 1, device_id=device, device_id_type=pl.DeviceIdType.MESH)

    for d in (4, 3, 5, 2, 6, 1, 7):
        greet(zdev(d))
    for d in PLANE:
        greet(pdev(d))
        greet(twin(d))
    greet(sibling)

    def remote(src, dst, send, recv, device):
        return pltpu.make_async_remote_copy(
            src_ref=src, dst_ref=dst, send_sem=send, recv_sem=recv,
            device_id=device, device_id_type=pl.DeviceIdType.MESH,
        )

    low = lax.broadcasted_iota(jnp.int32, (1, 128), 1) < COLS

    def swap(x):
        return pltpu.roll(x, COLS, 1)

    for load in loads:
        load.wait()
    for t in range(8):
        tile = jnp.concatenate([pair[t], pair[t + 8]], axis=0).astype(F32)
        state[:, t * 128:(t + 1) * 128] = tile.T
    for u in range(2):
        for n, ref in enumerate((in_gain, in_bias, out_gain, out_bias)):
            cols[u, n] = jnp.broadcast_to(column(ref[u:u + 1, :]), (C, 128))
        for g in range(5):
            wt[u, g * 128:(g + 1) * 128, :] = projection[u, :, g * 128:(g + 1) * 128].astype(F32).T.astype(BF16)
        wo[u] = out_weight[u].astype(F32).T.astype(BF16)

    def project(u, half):
        def one(t, _):
            lanes = pl.ds(pl.multiple_of((half * 4 + t) * 128, 128), 128)
            part_lanes = pl.ds(pl.multiple_of(t * 128, 128), 128)
            nrm = norm0(state[:, lanes], cols[u, 0], cols[u, 1]).astype(BF16)
            normed[:, lanes] = nrm
            proj = dot(wt[u, :512, :], nrm, ((1,), (0,)))
            left = (sigmoid(proj[128:256]) * proj[:128]).astype(BF16)
            right = (sigmoid(proj[384:512]) * proj[256:384]).astype(BF16)
            sa[u, half, :, 0:16, part_lanes] = left.reshape(NZ, 16, 128)
            sa[u, half, :, 16:32, part_lanes] = right.reshape(NZ, 16, 128)
            return 0

        lax.fori_loop(0, 4, one, 0, unroll=UNROLL)

    def send_z(u, half):
        for d in STEPS[1:]:
            to = ring_z[d]
            remote(sa.at[u, half, to], ra.at[u, half, z], s1.at[u, half, d], r1.at[u, half, z], zdev(d)).start()

    project(0, 0)
    pl.semaphore_wait(barrier, NZ - 1 + 2 * (NP - 1) + 1)
    send_z(0, 0)
    project(0, 1)
    send_z(0, 1)

    for u in range(2):
        def gates(t, _):
            lanes = pl.ds(pl.multiple_of(t * 128, 128), 128)
            gate[:, lanes] = sigmoid(dot(wt[u, 512:, :], normed[:, lanes], ((1,), (0,))))
            return 0

        lax.fori_loop(0, 8, gates, 0, unroll=UNROLL)

        def spread_out(s):
            zs = ring_z[STEPS[s]]
            for half in range(2):
                if s > 0:
                    remote(sa.at[u, half, zs], ra.at[u, half, zs], s1.at[u, half, 0], r1.at[u, half, zs], zdev(STEPS[s])).wait_recv()
                src = sa.at[u, half, zs] if s == 0 else ra.at[u, half, zs]
                for t in range(4):
                    vl = src[0:16, t * 128:(t + 1) * 128].astype(F32)
                    vr = src[16:32, t * 128:(t + 1) * 128].astype(F32)
                    n = half * 4 + t
                    spread[pl.ds(n, 16, stride=16), :] = jnp.where(low, vl, swap(vr))
                    spread[pl.ds(8 + n, 16, stride=16), :] = jnp.where(low, swap(vl), vr)
            sx[u, :, s] = spread[...].reshape(NP, 16, 128).astype(BF16)

        def send_plane(g):
            steps = part(g)
            here = (u, col, yh, core, steps)
            for d in PLANE:
                to = across(d)
                if g == NF - 1:
                    remote(sx.at[u, to, steps], rx.at[here], s3.at[u, g], r3.at[u, g], twin(d)).start()
                remote(sx.at[u, to, steps], rx.at[here], s2.at[u, g], r2.at[u, g], pdev(d)).start()
            if g == NF - 1:
                remote(sx.at[u, p, steps], rx.at[here], s3.at[u, g], r3.at[u, g], sibling).start()
            rx[u, col, yh, core, steps] = sx[u, p, steps]

        def swap_cores(g):
            steps = part(g)
            whole = rx.at[u, :, :, core, steps]
            most = sx.at[u, pl.ds(0, NP - 1), steps]
            pltpu.make_async_copy(most, most, r2.at[u, g]).wait()
            if g < NF - 1:
                remote(whole, whole, s3.at[u, g], r3.at[u, g], sibling).start()

        def build(g):
            steps = part(g)
            theirs = rx.at[u, :, :, 1 - core, steps]
            pltpu.make_async_copy(theirs, theirs, r3.at[u, g]).wait()
            for s in range(START[g], START[g + 1]):
                zs = ring_z[STEPS[s]]
                for h in range(2):
                    for k in range(2):
                        place = pl.ds(pl.multiple_of(((h * NZ + zs) * 2 + k) * 16, 16), 16)
                        for c in range(4):
                            x0 = rx[u, 2 * c, h, k, s].astype(F32)
                            x1 = rx[u, 2 * c + 1, h, k, s].astype(F32)
                            am[place, c * 128:(c + 1) * 128] = jnp.where(low, x0, swap(x1)).astype(BF16)
                            bm[place, c * 128:(c + 1) * 128] = jnp.where(low, swap(x0), x1).astype(BF16)

        for g in range(NF):
            for s in range(START[g], START[g + 1]):
                spread_out(s)
            send_plane(g)
            if g >= SWAP_LAG:
                swap_cores(g - SWAP_LAG)
        for g in range(max(0, NF - SWAP_LAG), NF - 1):
            swap_cores(g)
        swap_cores(NF - 1)
        for g in range(NF):
            build(g)

        if u == 1:
            def flip(i, _):
                lanes = pl.ds(pl.multiple_of(i * 128, 128), 128)
                for k in range(4):
                    at[lanes, k * 128:(k + 1) * 128] = am[k * 128:(k + 1) * 128, lanes].astype(F32).T.astype(BF16)
                return 0

            lax.fori_loop(0, 4, flip, 0)
        a_ref = am if u == 0 else at

        def triangle(g):
            rows = []
            for s in BACK[g * GROUP:(g + 1) * GROUP]:
                for h in range(2):
                    r = ((h * NZ + ring_z[s]) * 2 + core) * 16
                    rows.append(a_ref[pl.ds(pl.multiple_of(r, 16), 16), :])
            tri = dot(jnp.concatenate(rows, axis=0), bm[...], ((1,), (1 - u,)))
            for n in range(GROUP):
                for h in range(2):
                    for c in range(4):
                        block = tri[(n * 2 + h) * 16:(n * 2 + h + 1) * 16, c * 128:(c + 1) * 128]
                        first = jnp.where(low, block[0:8], swap(block[8:16]))
                        second = jnp.where(low, swap(block[0:8]), block[8:16])
                        at_row = (g * GROUP + n) * 4
                        for half in range(2):
                            rows4 = slice(half * 4, half * 4 + 4)
                            ts[half, 4 * c + 2 * h, at_row:at_row + 4] = first[rows4]
                            ts[half, 4 * c + 2 * h + 1, at_row:at_row + 4] = second[rows4]

        def send_back(half):
            tx[u, half] = ts[half].astype(BF16)
            for d in PLANE:
                to = across(d)
                remote(tx.at[u, half, to], ty.at[u, half, p], s4.at[u, half], r4.at[u, half], pdev(d)).start()
            ty[u, half, p] = tx[u, half, p]

        def gather_back(half):
            most = ty.at[u, half, pl.ds(0, NP - 1)]
            pltpu.make_async_copy(most, most, r4.at[u, half]).wait()
            for h in range(NP):
                spread2[pl.ds(h, 32, stride=16), :] = ty[u, half, h].astype(F32)
            for n in range(NZ):
                d = BACK[n]
                for t in range(4):
                    at_row = (n * 4 + t) * 16
                    tile = spread2[at_row:at_row + 16, :].astype(BF16)
                    if d == 0:
                        tf[u, half, z, :, t * 128:(t + 1) * 128] = tile
                    else:
                        tz[u, half, d, :, t * 128:(t + 1) * 128] = tile
                if d:
                    remote(tz.at[u, half, d], tf.at[u, half, z], s5.at[u, half, d], r5.at[u, half, z], zdev(d)).start()

        def wait_back(half):
            for d in range(1, NZ):
                zs = ring_z[d]
                remote(tz.at[u, half, d], tf.at[u, half, zs], s5.at[u, half, d], r5.at[u, half, zs], zdev(d)).wait_recv()

        def finish(half):
            def one(t, _):
                lanes = pl.ds(pl.multiple_of((half * 4 + t) * 128, 128), 128)
                tri = tf[u, half, :, :, pl.ds(pl.multiple_of(t * 128, 128), 128)].reshape(H, 128).astype(F32)
                nrm = norm0(tri, cols[u, 2], cols[u, 3]).astype(BF16)
                delta = dot(wo[u], nrm, ((1,), (0,)))
                new = state[:, lanes] + gate[:, lanes] * delta
                if u == 0:
                    state[:, lanes] = new.astype(BF16).astype(F32)
                else:
                    tile = new.T.astype(BF16)
                    updated[half * 4 + t] = tile[0:COLS]
                    updated[half * 4 + t + 8] = tile[COLS:]
                return 0

            lax.fori_loop(0, 4, one, 0, unroll=UNROLL)

        for g in range(NG):
            triangle(g)
        for half in range(2):
            send_back(half)
        for half in range(2):
            gather_back(half)
        for half in range(2):
            wait_back(half)
            finish(half)
            if u == 0:
                project(1, half)
                send_z(1, half)

    for u in range(2):
        for half in range(2):
            for d in range(1, NZ):
                zs = ring_z[d]
                remote(sa.at[u, half, zs], ra.at[u, half, z], s1.at[u, half, d], r1.at[u, half, z], zdev(d)).wait_send()
                remote(tz.at[u, half, d], tf.at[u, half, z], s5.at[u, half, d], r5.at[u, half, z], zdev(d)).wait_send()
            sent = tx.at[u, half, pl.ds(0, NP - 1)]
            pltpu.make_async_copy(sent, sent, s4.at[u, half]).wait()
        for g in range(NF):
            sent = sx.at[u, pl.ds(0, NP - 1), part(g)]
            pltpu.make_async_copy(sent, sent, s2.at[u, g]).wait()
            sent = sx.at[u, :, part(g)] if g == NF - 1 else rx.at[u, :, :, core, part(g)]
            pltpu.make_async_copy(sent, sent, s3.at[u, g]).wait()


def local(pair, in_gain, in_bias, projection, out_gain, out_bias, out_weight):
    vm = pltpu.VMEM
    dma = pltpu.SemaphoreType.DMA
    return pl.pallas_call(
        kernel,
        out_shape=jax.ShapeDtypeStruct((ROWS, COLS, C), BF16),
        in_specs=[pl.BlockSpec(memory_space=pltpu.HBM)] * 7,
        out_specs=pl.BlockSpec(memory_space=vm),
        scratch_shapes=[
            vm((ROWS, COLS, C), BF16),
            vm((2, C), F32),
            vm((2, C), F32),
            vm((2, C, 640), BF16),
            vm((2, H), F32),
            vm((2, H), F32),
            vm((2, H, C), BF16),
            dma((7,)),
            vm((C, LANES), F32),
            vm((C, LANES), BF16),
            vm((C, LANES), F32),
            vm((2, 4, C, 128), F32),
            vm((2, 640, C), BF16),
            vm((2, C, H), BF16),
            vm((2, 2, NZ, 32, HALF), BF16),
            vm((2, 2, NZ, 32, HALF), BF16),
            vm((256, 128), F32),
            vm((2, NP, NZ, 16, 128), BF16),
            vm((2, 8, 2, 2, NZ, 16, 128), BF16),
            vm((512, 512), BF16),
            vm((512, 512), BF16),
            vm((512, 512), BF16),
            vm((2, NP, 32, 128), F32),
            vm((2, 2, NP, 32, 128), BF16),
            vm((2, 2, NP, 32, 128), BF16),
            vm((512, 128), F32),
            vm((2, 2, NZ, 16, HALF), BF16),
            vm((2, 2, NZ, 16, HALF), BF16),
            dma((2, 2, NZ)), dma((2, 2, NZ)),
            dma((2, NF)), dma((2, NF)),
            dma((2, NF)), dma((2, NF)),
            dma((2, 2)), dma((2, 2)),
            dma((2, 2, NZ)), dma((2, 2, NZ)),
        ],
        compiler_params=pltpu.CompilerParams(
            collective_id=0, has_side_effects=True, vmem_limit_bytes=62 * 1024 * 1024
        ),
    )(pair, in_gain, in_bias, projection, out_gain, out_bias, out_weight)


def solution(mesh):
    return jax.shard_map(
        local,
        mesh=mesh,
        in_specs=(P("row", "col", None), P(), P(), P(), P(), P(), P()),
        out_specs=P("row", "col", None),
        check_vma=False,
    )
```
